128 devices in a mesh: kx: 16 (over z, y_lo, core), ky: 8 (over x, y_hi).
Axes of the slice: x: 4, y: 4 (y_hi: 2, y_lo: 2; y = y_hi * 2 + y_lo), z: 4, core: 2. Of those that a mesh axis runs over, the one named last changes fastest.
Arguments:
- kspace: bfloat16 [64, 32, 128, 256], P(None, 'kx', 'ky'), may hold values from -6 to 6
- kernel: bfloat16 [3, 3, 3, 64, 128], replicated, may hold values from -0.109375 to 0.109375
- mask: int32 [128, 256], P('ky'), may hold values 0 or 1
Outputs:
- updated: bfloat16 [64, 32, 128, 256], P(None, 'kx', 'ky')
- residual: bfloat16 [64, 32, 128, 256], P(None, 'kx', 'ky')
The draws below stay inside these ranges and needn't reach their ends.
All inputs are finite; a program needn't handle non-finite values. No bound on the sum of `mask` on one device may be relied on, other than what follows from the above.
Results may differ from the reference program's by a relative error of at most 0.0042.
Values may be sent and summed in bfloat16 or wider, within the bound.
A program may use at most 128 MiB of HBM per device.

```python
import jax
import jax.numpy as jnp

CH = 64
NZ = 256
NX = 32
NY = 128


def with_ends(array, key, low, high):
    longest = array.shape.index(max(array.shape))
    spots = []
    for shift in (0, 1):
        where = [jax.random.randint(jax.random.fold_in(key, axis), (), 0, length) for axis, length in enumerate(array.shape)]
        where[longest] = (where[longest] + shift) % array.shape[longest]
        spots.append(tuple(where))
    return array.at[spots[0]].set(low).at[spots[1]].set(high)


def level_of(key, dims, shards, smallest, largest):
    def one(axis_at, shards_of):
        heights = jax.random.uniform(jax.random.fold_in(jax.random.fold_in(key, 6), axis_at), (shards_of,), jnp.float32, smallest / len(shards), largest / len(shards))
        return jnp.repeat(jnp.exp(heights), dims[axis_at] // shards_of).reshape((-1,) + (1,) * (len(dims) - axis_at - 1))

    gain = one(*shards[0])
    for cut in shards[1:]:
        gain = gain * one(*cut)
    return gain


def normal_values(stream_key, extent, spread, most, shards=(), dtype=jnp.bfloat16):
    values = spread * jax.random.normal(stream_key, extent, jnp.float32)
    if shards:
        values = values * level_of(stream_key, extent, shards, -0.22, 0.18)
    return jnp.clip(values, -most, most).astype(dtype)


def setup_inputs(seed: int = 0) -> dict:
    arg_keys = jax.random.split(jax.random.key(seed), 4)
    return {
        "kspace": normal_values(arg_keys[0], (CH, NX, NY, NZ), 1.0, 6.0, ((1, 16), (2, 8))),
        "kernel": normal_values(arg_keys[1], (3, 3, 3, CH, 2 * CH), (54 * CH) ** -0.5, 0.109375),
        "mask": with_ends((jax.random.randint(arg_keys[2], (NY, NZ), 0, 3) < 1).astype(jnp.int32), jax.random.fold_in(arg_keys[2], 1), 0, 1),
    }


step_size = 0.5


def channel_signs(count):
    half = count // 2
    return jnp.concatenate([jnp.ones((half,), jnp.float32), -jnp.ones((count - half,), jnp.float32)])


def forward_sum(extended, kernel):
    padded = jnp.pad(extended.astype(jnp.float32), ((0, 0), (1, 1), (1, 1), (1, 1)))
    total = jnp.zeros((CH, NX, NY, NZ), jnp.float32)
    for first in range(3):
        for second in range(3):
            for third in range(3):
                window = padded[:, first:first + NX, second:second + NY, third:third + NZ]
                weights = kernel[first, second, third].astype(jnp.float32)
                total = total + jnp.einsum("oi,ixyz->oxyz", weights, window)
    return total


def adjoint_sum(residual, kernel):
    padded = jnp.pad(residual.astype(jnp.float32), ((0, 0), (1, 1), (1, 1), (1, 1)))
    total = jnp.zeros((2 * CH, NX, NY, NZ), jnp.float32)
    for first in range(3):
        for second in range(3):
            for third in range(3):
                window = padded[:, 2 - first:2 - first + NX, 2 - second:2 - second + NY, 2 - third:2 - third + NZ]
                weights = kernel[first, second, third].astype(jnp.float32)
                total = total + jnp.einsum("oi,oxyz->ixyz", weights, window)
    return total


def reference(kspace, kernel, mask):
    signs = channel_signs(CH)[:, None, None, None]
    virtual = (signs * kspace[:, ::-1, ::-1, ::-1].astype(jnp.float32)).astype(jnp.bfloat16)
    extended = jnp.concatenate([kspace, virtual], axis=0)
    residual = (forward_sum(extended, kernel) - kspace.astype(jnp.float32)).astype(jnp.bfloat16)
    adjoint = adjoint_sum(residual, kernel)
    back = adjoint[CH:].astype(jnp.bfloat16)
    gradient = adjoint[:CH] - residual.astype(jnp.float32) + signs * back[:, ::-1, ::-1, ::-1].astype(jnp.float32)
    keep = 1.0 - mask.astype(jnp.float32)
    updated = (kspace.astype(jnp.float32) - step_size * keep[None, None] * gradient).astype(jnp.bfloat16)
    return updated, residual
```

```python
import functools

import jax
import jax.numpy as jnp
from jax import lax
from jax.experimental import pallas as pl
from jax.experimental.pallas import tpu as pltpu
from jax.sharding import PartitionSpec as P

MESH = pl.DeviceIdType.MESH
BF = jnp.bfloat16
F32 = jnp.float32
CH = 64
NZ = 256
ROWS = 16
STEP = 0.5


A, B, LO, HI = (2, 8), (10, 8), (0, 2), (18, 2)


def shift_sum(terms, m):
    lane = lax.broadcasted_iota(jnp.int32, (m, NZ), 1)
    before = jnp.where(lane == 0, 0.0, pltpu.roll(terms[:m], 1, 1))
    after = jnp.where(lane == NZ - 1, 0.0, pltpu.roll(terms[2 * m :], NZ - 1, 1))
    return terms[m : 2 * m] + before + after


def build_weights(kernel_ref, wf, wa):
    lane = lax.broadcasted_iota(jnp.int32, (CH, 2 * CH), 1)
    sign = jnp.where(lane < CH + CH // 2, 1.0, -1.0)
    for i in range(3):
        for j in range(3):
            col = (i * 3 + j) * 2 * CH
            for l in range(3):
                here = kernel_ref[i, j, l].astype(F32) * sign
                there = kernel_ref[2 - i, 2 - j, 2 - l].astype(F32) * sign
                wf[l * 128 : l * 128 + 64, col : col + 128] = here.astype(BF)
                wf[l * 128 + 64 : l * 128 + 128, col : col + 128] = pltpu.roll(there, CH, 1).astype(BF)
                both = jnp.concatenate([there, pltpu.roll(here, CH, 1)], axis=0)
                wa[l * 64 : l * 64 + 64, col : col + 128] = jnp.transpose(both)[:CH].astype(BF)


def body(nx, ny, k_ref, kernel_ref, mask_ref, upd_ref, out_ref, ext, stage, res, wf, wa, flip, lsem, ssem, rsem):
    a = lax.axis_index("kx")
    b = lax.axis_index("ky")
    core = lax.rem(a, 2)
    side = 2 * core - 1
    has_n = jnp.logical_and(a > 0, a < nx - 1)
    has_u = b < ny - 1
    has_d = b > 0
    dev_p = (a + 1 - 2 * core, b)
    dev_n = (jnp.clip(a + side, 0, nx - 1), b)
    dev_m = (nx - 1 - a, ny - 1 - b)
    dev_u = (a, jnp.minimum(b + 1, ny - 1))
    dev_d = (a, jnp.maximum(b - 1, 0))

    def plane_of(s):
        return (1 - s) + core * (2 * s - 1)

    own = []
    for s in (0, 1):
        cp = pltpu.make_async_copy(
            k_ref.at[plane_of(s)], ext.at[s + 1, 2:18, 0:64], lsem.at[s]
        )
        cp.start()
        own.append(cp)

    barrier = pltpu.get_barrier_semaphore()

    def greet(dev):
        pl.semaphore_signal(barrier, inc=1, device_id=dev, device_id_type=MESH)

    greet(dev_p)
    greet(dev_m)
    for ok, dev in ((has_n, dev_n), (has_u, dev_u), (has_d, dev_d)):

        @pl.when(ok)
        def _(dev=dev):
            greet(dev)

    zero2 = jnp.zeros((2, 2, CH, NZ), BF)

    @pl.when(jnp.logical_not(has_d))
    def _():
        ext[1:3, 0:2, 0:64, :] = zero2

    @pl.when(jnp.logical_not(has_u))
    def _():
        ext[1:3, 18:20, 0:64, :] = zero2

    @pl.when(jnp.logical_not(has_n))
    def _():
        def clear(i, carry):
            ext[3 + i // 20, i % 20] = jnp.zeros((2 * CH, NZ), BF)
            return carry

        lax.fori_loop(0, 40, clear, 0)

    for cp in own:
        cp.wait()
    pl.semaphore_wait(
        barrier, 2 + has_n.astype(jnp.int32) + has_u.astype(jnp.int32) + has_d.astype(jnp.int32)
    )

    counter = [0]
    sends = []

    def remote(src, dst, dev, ok=None, rok=None):
        k = counter[0]
        counter[0] += 1
        cp = pltpu.make_async_remote_copy(
            src_ref=src, dst_ref=dst, send_sem=ssem.at[k], recv_sem=rsem.at[k],
            device_id=dev, device_id_type=MESH,
        )
        rok = ok if rok is None else rok
        if ok is None:
            cp.start()
        else:
            pl.when(ok)(cp.start)
        sends.append((cp, ok))

        def arrived():
            if rok is None:
                cp.wait_recv()
            else:
                pl.when(rok)(cp.wait_recv)

        return arrived

    def k_rows(e, part):
        return ext.at[e, part[0] : part[0] + part[1], 0:64]

    def m_rows(e, part):
        return ext.at[e, part[0] : part[0] + part[1], 64:128]

    def s_rows(slot, part):
        return stage.at[slot, part[0] : part[0] + part[1]]

    def to_n(rows, e, part):
        return remote(rows(e, part), rows(5 - e, part), dev_n, has_n)

    def to_p(rows, part):
        return remote(rows(1, part), rows(0, part), dev_p)

    def to_m(e, part, ok=None):
        return remote(k_rows(e, part), s_rows({1: 0, 2: 1, 4: 2}[e], part), dev_m, ok)

    from_d = remote(ext.at[1:3, 16:18, 0:64], ext.at[1:3, 0:2, 0:64], dev_u, has_u, has_d)
    from_u = remote(ext.at[1:3, 2:4, 0:64], ext.at[1:3, 18:20, 0:64], dev_d, has_d, has_u)
    m_a = [to_m(1, B), to_m(2, B)]
    n_k2 = [to_n(k_rows, 2, part) for part in (A, B)]
    m_b = [to_m(1, A), to_m(2, A)]
    p_k = [to_p(k_rows, part) for part in (A, B)]
    n_k1 = [to_n(k_rows, 1, part) for part in (B, A)]

    build_weights(kernel_ref, wf, wa)
    row_id = lax.broadcasted_iota(jnp.int32, (NZ, NZ), 0)
    col_id = lax.broadcasted_iota(jnp.int32, (NZ, NZ), 1)
    flip[...] = jnp.where(row_id + col_id == NZ - 1, 1.0, 0.0).astype(BF)

    def turn(slot, e, part):
        start, count = part

        def pair(i, carry):
            t = start + 2 * i
            two = stage[slot, pl.ds(18 - t, 2)].reshape(2 * CH, NZ)
            back = jnp.dot(two, flip[...], preferred_element_type=F32).astype(BF)
            ext[e, t, 64:128, :] = back[CH:]
            ext[e, t + 1, 64:128, :] = back[:CH]
            return carry

        lax.fori_loop(0, count // 2, pair, 0, unroll=count // 2)

    def forward_row(s, j):
        rhs = jnp.concatenate(
            [ext[s + 1 + side * d, pl.ds(j, 3)].reshape(6 * CH, NZ) for d in (-1, 0, 1)], axis=0
        )
        terms = jnp.dot(wf[...], rhs, preferred_element_type=F32)
        total = shift_sum(terms, 2 * CH) - ext[s + 1, j + 1].astype(F32)
        res[s + 1, j] = total.astype(BF)

    def forward(s, start, count):
        def step(i, carry):
            forward_row(s, start + i)
            return carry

        lax.fori_loop(0, count, step, 0, unroll=2)

    def forward_edges(s):
        def step(i, carry):
            forward_row(s, i + 14 * (i // 2))
            return carry

        lax.fori_loop(0, 4, step, 0, unroll=2)

        @pl.when(jnp.logical_not(has_d))
        def _():
            res[s + 1, 0] = jnp.zeros((2 * CH, NZ), BF)

        @pl.when(jnp.logical_not(has_u))
        def _():
            res[s + 1, 17] = jnp.zeros((2 * CH, NZ), BF)

    def adjoint(s, start, count):
        plane = plane_of(s)

        def step(i, carry):
            y = start + i
            rhs = jnp.concatenate(
                [res[s + 1 + side * d, pl.ds(y, 3)].reshape(6 * CH, NZ) for d in (-1, 0, 1)], axis=0
            )
            terms = jnp.dot(wa[...], rhs, preferred_element_type=F32)
            own_r = res[s + 1, y + 1, 0:64]
            gradient = shift_sum(terms, CH) - own_r.astype(F32)
            keep = 1.0 - mask_ref[pl.ds(y, 1), :].astype(F32)
            new = ext[s + 1, y + 2, 0:64].astype(F32) - (STEP * keep) * gradient
            upd_ref[plane, y] = new.astype(BF)
            out_ref[plane, y] = own_r
            return carry

        lax.fori_loop(0, count, step, 0, unroll=2)

    from_d()
    from_u()
    m_l = [to_m(e, part) for part in (HI, LO) for e in (1, 2)]
    n_e2 = [to_n(k_rows, 2, part) for part in (LO, HI)]
    n_e1 = [to_n(k_rows, 1, part) for part in (HI, LO)]
    p_e = [to_p(k_rows, part) for part in (LO, HI)]

    for got in m_a:
        got()
    turn(0, 1, A)
    turn(1, 2, A)
    n_ma = to_n(m_rows, 2, A)
    p_ma = to_p(m_rows, A)
    for got in p_k:
        got()
    p_ma()
    forward(0, 2, 6)
    for got in m_b:
        got()
    turn(0, 1, B)
    turn(1, 2, B)
    n_mb = to_n(m_rows, 2, B)
    p_mb = to_p(m_rows, B)
    n_k1[0]()
    f_a = to_m(4, B, has_n)
    n_k1[1]()
    f_b = to_m(4, A, has_n)
    p_mb()
    forward(0, 8, 8)
    for got in m_l:
        got()
    for part in (LO, HI):
        turn(0, 1, part)
        turn(1, 2, part)
    n_ml = [to_n(m_rows, 2, part) for part in (LO, HI)]
    p_ml = [to_p(m_rows, part) for part in (LO, HI)]
    for got in n_e1:
        got()
    f_l = [to_m(4, part, has_n) for part in (HI, LO)]
    for got in p_e + p_ml:
        got()
    forward_edges(0)
    r_p = remote(res.at[1], res.at[0], dev_p)
    for got in n_k2:
        got()
    n_ma()
    forward(1, 2, 6)

    def when_n(fn):
        pl.when(has_n)(fn)

    f_a()
    when_n(lambda: turn(2, 4, A))
    when_n(lambda: forward(2, 2, 6))
    n_mb()
    forward(1, 8, 8)
    f_b()
    when_n(lambda: turn(2, 4, B))
    when_n(lambda: forward(2, 8, 8))
    r_p()
    adjoint(0, 2, 12)
    for got in n_e2 + n_ml:
        got()
    forward_edges(1)
    for got in f_l:
        got()

    def last():
        turn(2, 4, LO)
        turn(2, 4, HI)
        forward_edges(2)

    when_n(last)

    @pl.when(jnp.logical_not(has_n))
    def _():
        def clear(i, carry):
            res[3, i] = jnp.zeros((2 * CH, NZ), BF)
            return carry

        lax.fori_loop(0, 18, clear, 0)

    adjoint(0, 0, 2)
    adjoint(0, 14, 2)
    adjoint(1, 0, 16)
    for cp, ok in sends:
        if ok is None:
            cp.wait_send()
        else:
            pl.when(ok)(cp.wait_send)


N_COPIES = 35


def gradient_step(nx, ny, planes_first, kernel, mask):
    vmem = pl.BlockSpec(memory_space=pltpu.VMEM)
    shape = jax.ShapeDtypeStruct((2, ROWS, CH, NZ), BF)
    return pl.pallas_call(
        functools.partial(body, nx, ny),
        out_shape=(shape, shape),
        in_specs=[pl.BlockSpec(memory_space=pl.ANY), vmem, vmem],
        out_specs=(vmem, vmem),
        scratch_shapes=[
            pltpu.VMEM((5, 20, 2 * CH, NZ), BF),
            pltpu.VMEM((3, 20, CH, NZ), BF),
            pltpu.VMEM((4, 18, 2 * CH, NZ), BF),
            pltpu.VMEM((6 * CH, 18 * CH), BF),
            pltpu.VMEM((3 * CH, 18 * CH), BF),
            pltpu.VMEM((NZ, NZ), BF),
            pltpu.SemaphoreType.DMA((2,)),
            pltpu.SemaphoreType.DMA((N_COPIES,)),
            pltpu.SemaphoreType.DMA((N_COPIES,)),
        ],
        compiler_params=pltpu.CompilerParams(
            collective_id=0, has_side_effects=True, vmem_limit_bytes=48 << 20
        ),
        name="gradient_step",
    )(planes_first, kernel, mask)


def local(nx, ny, kspace, kernel, mask):
    planes_first = jnp.transpose(kspace, (1, 2, 0, 3))
    updated, residual = gradient_step(nx, ny, planes_first, kernel, mask)
    return (
        jnp.transpose(updated, (2, 0, 1, 3)),
        jnp.transpose(residual, (2, 0, 1, 3)),
    )


def solution(mesh):
    nx, ny = mesh.shape["kx"], mesh.shape["ky"]
    return jax.shard_map(
        functools.partial(local, nx, ny),
        mesh=mesh,
        in_specs=(P(None, "kx", "ky", None), P(), P("ky", None)),
        out_specs=(P(None, "kx", "ky", None), P(None, "kx", "ky", None)),
        check_vma=False,
    )
```

```python
import functools

import jax
import jax.numpy as jnp
from jax import lax
from jax.experimental import pallas as pl
from jax.experimental.pallas import tpu as pltpu
from jax.sharding import PartitionSpec as P

MESH = pl.DeviceIdType.MESH
BF = jnp.bfloat16
F32 = jnp.float32
CH = 64
NZ = 256
ROWS = 16
STEP = 0.5


UPPER, LOWER, EDGE = (6, 6), (2, 4), (0, 2)
MAIN = (2, 10)


def shift_sum(terms, m):
    lane = lax.broadcasted_iota(jnp.int32, (m, NZ), 1)
    before = jnp.where(lane == 0, 0.0, pltpu.roll(terms[:m], 1, 1))
    after = jnp.where(lane == NZ - 1, 0.0, pltpu.roll(terms[2 * m :], NZ - 1, 1))
    return terms[m : 2 * m] + before + after


def build_weights(kernel_ref, wf, wa):
    lane = lax.broadcasted_iota(jnp.int32, (CH, 2 * CH), 1)
    sign = jnp.where(lane < CH + CH // 2, 1.0, -1.0)
    for i in range(3):
        for j in range(3):
            col = (i * 3 + j) * 2 * CH
            for l in range(3):
                here = kernel_ref[i, j, l].astype(F32) * sign
                there = kernel_ref[2 - i, 2 - j, 2 - l].astype(F32) * sign
                wf[l * 128 : l * 128 + 64, col : col + 128] = here.astype(BF)
                wf[l * 128 + 64 : l * 128 + 128, col : col + 128] = pltpu.roll(there, CH, 1).astype(BF)
                both = jnp.concatenate([there, pltpu.roll(here, CH, 1)], axis=0)
                wa[l * 128 : l * 128 + 128, col : col + 128] = jnp.transpose(both).astype(BF)


def body(
    nx, ny, k_ref, kernel_ref, mask_ref, upd_ref, out_ref,
    ext, whole, stage, res, step_m, back_r, back_u, wf, wa, flip, lsem, ssem, rsem,
):
    a = lax.axis_index("kx")
    b = lax.axis_index("ky")
    core = lax.rem(a, 2)
    side = 2 * core - 1
    has_n = jnp.logical_and(a > 0, a < nx - 1)
    has_u = b < ny - 1
    has_d = b > 0
    dev_p = (a + 1 - 2 * core, b)
    dev_n = (jnp.clip(a + side, 0, nx - 1), b)
    dev_m = (nx - 1 - a, ny - 1 - b)
    dev_u = (a, jnp.minimum(b + 1, ny - 1))
    dev_d = (a, jnp.maximum(b - 1, 0))

    def plane_of(s):
        return (1 - s) + core * (2 * s - 1)

    own = []
    for s in (0, 1):
        for src, dst in (
            (k_ref.at[plane_of(s)], whole.at[s, 2:18]),
            (k_ref.at[plane_of(s), 0:10], ext.at[s + 1, 2:12, 0:64]),
        ):
            cp = pltpu.make_async_copy(src, dst, lsem.at[len(own)])
            cp.start()
            own.append(cp)

    barrier = pltpu.get_barrier_semaphore()

    def greet(dev):
        pl.semaphore_signal(barrier, inc=1, device_id=dev, device_id_type=MESH)

    greet(dev_p)
    greet(dev_m)
    for ok, dev in ((has_n, dev_n), (has_u, dev_u), (has_d, dev_d)):

        @pl.when(ok)
        def _(dev=dev):
            greet(dev)

    zero2 = jnp.zeros((2, 2, CH, NZ), BF)

    @pl.when(jnp.logical_not(has_d))
    def _():
        ext[1:3, 0:2, 0:64, :] = zero2

    @pl.when(jnp.logical_not(has_u))
    def _():
        whole[:, 18:20] = zero2

    @pl.when(jnp.logical_not(has_n))
    def _():
        def clear(i, carry):
            ext[3, i] = jnp.zeros((2 * CH, NZ), BF)
            return carry

        lax.fori_loop(0, 12, clear, 0)

        def clear_res(i, carry):
            res[3, i] = jnp.zeros((2 * CH, NZ), BF)
            return carry

        lax.fori_loop(0, 10, clear_res, 0)

    for cp in own:
        cp.wait()
    pl.semaphore_wait(barrier, 2 + sum(ok.astype(jnp.int32) for ok in (has_n, has_u, has_d)))

    counter = [0]
    sends = []

    def remote(src, dst, dev, ok=None, rok=None):
        k = counter[0]
        counter[0] += 1
        cp = pltpu.make_async_remote_copy(
            src_ref=src, dst_ref=dst, send_sem=ssem.at[k], recv_sem=rsem.at[k],
            device_id=dev, device_id_type=MESH,
        )
        rok = ok if rok is None else rok
        if ok is None:
            cp.start()
        else:
            pl.when(ok)(cp.start)
        sends.append((cp, ok))

        def arrived():
            if rok is None:
                cp.wait_recv()
            else:
                pl.when(rok)(cp.wait_recv)

        return arrived

    def k_rows(e, part):
        return ext.at[e, part[0] : part[0] + part[1], 0:64]

    def m_rows(e, part):
        return ext.at[e, part[0] : part[0] + part[1], 64:128]

    def to_n(rows, e, part):
        return remote(rows(e, part), rows(5 - e, part), dev_n, has_n)

    def to_p(rows, part):
        return remote(rows(1, part), rows(0, part), dev_p)

    def to_m(part):
        first = 12 - part[0] - part[1]
        return remote(
            whole.at[0:2, 8 + first : 8 + first + part[1]],
            stage.at[0:2, first : first + part[1]],
            dev_m,
        )

    from_d = remote(whole.at[0:2, 16:18], ext.at[1:3, 0:2, 0:64], dev_u, has_u, has_d)
    from_u = remote(whole.at[0:2, 2:4], whole.at[0:2, 18:20], dev_d, has_d, has_u)
    m_upper = to_m(UPPER)
    m_lower = to_m(LOWER)
    n_k = [to_n(k_rows, e, MAIN) for e in (2, 1)]
    p_k = to_p(k_rows, MAIN)

    build_weights(kernel_ref, wf, wa)
    row_id = lax.broadcasted_iota(jnp.int32, (NZ, NZ), 0)
    col_id = lax.broadcasted_iota(jnp.int32, (NZ, NZ), 1)
    flip[...] = jnp.where(row_id + col_id == NZ - 1, 1.0, 0.0).astype(BF)

    def turned(two):
        return jnp.dot(two.reshape(2 * CH, NZ), flip[...], preferred_element_type=F32)

    def turn(part):
        start, count = part
        for s in (0, 1):

            def pair(i, carry, s=s):
                t = start + 2 * i
                back = turned(stage[s, pl.ds(10 - t, 2)]).astype(BF)
                ext[s + 1, t, 64:128, :] = back[CH:]
                ext[s + 1, t + 1, 64:128, :] = back[:CH]
                return carry

            lax.fori_loop(0, count // 2, pair, 0, unroll=count // 2)

    def forward(s, start, count):
        def step(i, carry):
            j = start + i
            rhs = jnp.concatenate(
                [ext[s + 1 + side * d, pl.ds(j, 3)].reshape(6 * CH, NZ) for d in (-1, 0, 1)], axis=0
            )
            terms = jnp.dot(wf[...], rhs, preferred_element_type=F32)
            total = shift_sum(terms, 2 * CH) - ext[s + 1, j + 1].astype(F32)
            res[s + 1, j] = total.astype(BF)
            return carry

        lax.fori_loop(0, count, step, 0, unroll=count)

    def forward_edge(s):
        forward(s, 0, 2)

        @pl.when(jnp.logical_not(has_d))
        def _():
            res[s + 1, 0] = jnp.zeros((2 * CH, NZ), BF)

    def adjoint(s, start, count):
        plane = plane_of(s)

        def step(i, carry):
            y = start + i
            rhs = jnp.concatenate(
                [res[s + 1 + side * d, pl.ds(y, 3)].reshape(6 * CH, NZ) for d in (-1, 0, 1)], axis=0
            )
            terms = jnp.dot(wa[...], rhs, preferred_element_type=F32)
            r = res[s + 1, y + 1]
            gradient = shift_sum(terms, 2 * CH) - r.astype(F32)
            k = ext[s + 1, y + 2].astype(F32)
            keep = 1.0 - mask_ref[pl.ds(y, 1), :].astype(F32)
            new = k[:CH] - (STEP * keep) * gradient[:CH]
            upd_ref[plane, y] = new.astype(BF)
            out_ref[plane, y] = r[:CH]
            step_m[s, y] = (k[CH:] - STEP * gradient[CH:]).astype(BF)
            return carry

        lax.fori_loop(0, count, step, 0, unroll=count)

    def return_r(s, start, count):
        return remote(
            res.at[s + 1, start + 1 : start + 1 + count, 64:128],
            back_r.at[s, start : start + count],
            dev_m,
        )

    def return_u(s, start, count):
        return remote(
            step_m.at[s, start : start + count], back_u.at[s, start : start + count], dev_m
        )

    def take_r(s, start, count):
        plane = plane_of(s)

        def pair(i, carry):
            q = start + 2 * i
            back = turned(back_r[s, pl.ds(q, 2)]).astype(BF)
            out_ref[plane, 15 - q] = back[:CH]
            out_ref[plane, 14 - q] = back[CH:]
            return carry

        lax.fori_loop(0, count // 2, pair, 0, unroll=count // 2)

    def take_u(s, start, count):
        plane = plane_of(s)

        def pair(i, carry):
            q = start + 2 * i
            back = turned(back_u[s, pl.ds(q, 2)])
            for n in (0, 1):
                y = 15 - q - n
                masked = jnp.broadcast_to(mask_ref[pl.ds(y, 1), :], (CH, NZ)) > 0
                k = whole[s, y + 2].astype(F32)
                upd_ref[plane, y] = jnp.where(masked, k, back[n * CH : n * CH + CH]).astype(BF)
            return carry

        lax.fori_loop(0, count // 2, pair, 0, unroll=count // 2)

    def when_n(fn, *args):
        pl.when(has_n)(lambda: fn(*args))

    from_d()
    n_k += [to_n(k_rows, e, EDGE) for e in (2, 1)]
    p_k_edge = to_p(k_rows, EDGE)
    from_u()
    m_edge = to_m(EDGE)

    m_upper()
    turn(UPPER)
    n_upper = [to_n(m_rows, e, UPPER) for e in (2, 1)]
    p_upper = to_p(m_rows, UPPER)
    m_lower()
    turn(LOWER)
    n_lower = [to_n(m_rows, e, LOWER) for e in (2, 1)]
    p_lower = to_p(m_rows, LOWER)
    p_k()
    p_upper()
    forward(0, 6, 4)
    m_edge()
    turn(EDGE)
    n_edge = [to_n(m_rows, e, EDGE) for e in (2, 1)]
    p_edge = to_p(m_rows, EDGE)
    p_lower()
    forward(0, 2, 4)
    p_k_edge()
    p_edge()
    forward_edge(0)
    r_p = remote(res.at[1], res.at[0], dev_p)
    r_0 = return_r(0, 0, 8)

    for got in n_k:
        got()
    n_upper[0]()
    forward(1, 6, 4)
    n_upper[1]()
    when_n(forward, 2, 6, 4)
    r_p()
    adjoint(0, 6, 2)
    adjoint(1, 6, 2)
    n_lower[0]()
    forward(1, 2, 4)
    r_1 = return_r(1, 2, 6)
    adjoint(0, 2, 4)
    u_0 = return_u(0, 2, 6)
    n_lower[1]()
    when_n(forward, 2, 2, 4)
    adjoint(1, 2, 4)
    u_1 = return_u(1, 2, 6)
    n_edge[0]()
    forward_edge(1)
    r_e = return_r(1, 0, 2)
    adjoint(0, 0, 2)
    u_0e = return_u(0, 0, 2)
    n_edge[1]()
    when_n(forward_edge, 2)
    adjoint(1, 0, 2)
    u_1e = return_u(1, 0, 2)

    r_0()
    take_r(0, 0, 8)
    r_1()
    take_r(1, 2, 6)
    u_0()
    take_u(0, 2, 6)
    u_1()
    take_u(1, 2, 6)
    r_e()
    take_r(1, 0, 2)
    u_0e()
    take_u(0, 0, 2)
    u_1e()
    take_u(1, 0, 2)
    for cp, ok in sends:
        if ok is None:
            cp.wait_send()
        else:
            pl.when(ok)(cp.wait_send)


N_COPIES = 28


def gradient_step(nx, ny, planes_first, kernel, mask):
    vmem = pl.BlockSpec(memory_space=pltpu.VMEM)
    shape = jax.ShapeDtypeStruct((2, ROWS, CH, NZ), BF)
    half = pltpu.VMEM((2, ROWS // 2, CH, NZ), BF)
    return pl.pallas_call(
        functools.partial(body, nx, ny),
        out_shape=(shape, shape),
        in_specs=[pl.BlockSpec(memory_space=pl.ANY), vmem, vmem],
        out_specs=(vmem, vmem),
        scratch_shapes=[
            pltpu.VMEM((5, 12, 2 * CH, NZ), BF),
            pltpu.VMEM((2, 20, CH, NZ), BF),
            pltpu.VMEM((2, 12, CH, NZ), BF),
            pltpu.VMEM((4, 10, 2 * CH, NZ), BF),
            half,
            half,
            half,
            pltpu.VMEM((6 * CH, 18 * CH), BF),
            pltpu.VMEM((6 * CH, 18 * CH), BF),
            pltpu.VMEM((NZ, NZ), BF),
            pltpu.SemaphoreType.DMA((4,)),
            pltpu.SemaphoreType.DMA((N_COPIES,)),
            pltpu.SemaphoreType.DMA((N_COPIES,)),
        ],
        compiler_params=pltpu.CompilerParams(
            collective_id=0, has_side_effects=True, vmem_limit_bytes=48 << 20
        ),
        name="gradient_step",
    )(planes_first, kernel, mask)


def local(nx, ny, kspace, kernel, mask):
    planes_first = jnp.transpose(kspace, (1, 2, 0, 3))
    updated, residual = gradient_step(nx, ny, planes_first, kernel, mask)
    return (
        jnp.transpose(updated, (2, 0, 1, 3)),
        jnp.transpose(residual, (2, 0, 1, 3)),
    )


def solution(mesh):
    nx, ny = mesh.shape["kx"], mesh.shape["ky"]
    return jax.shard_map(
        functools.partial(local, nx, ny),
        mesh=mesh,
        in_specs=(P(None, "kx", "ky", None), P(), P("ky", None)),
        out_specs=(P(None, "kx", "ky", None), P(None, "kx", "ky", None)),
        check_vma=False,
    )
```

```python
import functools

import jax
import jax.numpy as jnp
from jax import lax
from jax.experimental import pallas as pl
from jax.experimental.pallas import tpu as pltpu
from jax.sharding import PartitionSpec as P

MESH = pl.DeviceIdType.MESH
BF = jnp.bfloat16
F32 = jnp.float32
CH = 64
NZ = 256
ROWS = 16
STEP = 0.5


UPPER, LOWER, EDGE = (6, 6), (2, 4), (0, 2)
MAIN = (2, 10)


def shift_sum(terms, m):
    lane = lax.broadcasted_iota(jnp.int32, (m, NZ), 1)
    before = jnp.where(lane == 0, 0.0, pltpu.roll(terms[:m], 1, 1))
    after = jnp.where(lane == NZ - 1, 0.0, pltpu.roll(terms[2 * m :], NZ - 1, 1))
    return terms[m : 2 * m] + before + after


def build_weights(kernel_ref, wf, wa, side):
    lane = lax.broadcasted_iota(jnp.int32, (CH, 2 * CH), 1)
    sign = jnp.where(lane < CH + CH // 2, 1.0, -1.0)
    for i in range(3):
        plus, minus = 1 + side * (i - 1), 1 - side * (i - 1)
        for j in range(3):
            col = (i * 3 + j) * 2 * CH
            for l in range(3):
                here = kernel_ref[plus, j, l].astype(F32) * sign
                there = kernel_ref[minus, 2 - j, 2 - l].astype(F32) * sign
                wf[l * 128 : l * 128 + 64, col : col + 128] = here.astype(BF)
                wf[l * 128 + 64 : l * 128 + 128, col : col + 128] = pltpu.roll(there, CH, 1).astype(BF)
                both = jnp.concatenate([there, pltpu.roll(here, CH, 1)], axis=0)
                wa[l * 128 : l * 128 + 128, col : col + 128] = jnp.transpose(both).astype(BF)


def body(
    nx, ny, k_ref, kernel_ref, mask_ref, upd_ref, out_ref,
    ext, whole, stage, res, sum_f, sum_a, step_m, back_r, back_u, wf, wa, flip, lsem, ssem, rsem,
):
    a = lax.axis_index("kx")
    b = lax.axis_index("ky")
    core = lax.rem(a, 2)
    side = 2 * core - 1
    has_n = jnp.logical_and(a > 0, a < nx - 1)
    has_u = b < ny - 1
    has_d = b > 0
    dev_p = (a + 1 - 2 * core, b)
    dev_n = (jnp.clip(a + side, 0, nx - 1), b)
    dev_m = (nx - 1 - a, ny - 1 - b)
    middle = jnp.logical_or(a == nx // 2 - 1, a == nx // 2)
    outer = jnp.logical_and(has_n, jnp.logical_not(middle))
    dev_x = (nx - 1 - jnp.clip(a + side, 0, nx - 1), ny - 1 - b)
    dev_u = (a, jnp.minimum(b + 1, ny - 1))
    dev_d = (a, jnp.maximum(b - 1, 0))

    def plane_of(s):
        return (1 - s) + core * (2 * s - 1)

    own = []
    for s in (0, 1):
        for src, dst in (
            (k_ref.at[plane_of(s)], whole.at[s, 2:18]),
            (k_ref.at[plane_of(s), 0:10], ext.at[s + 1, 2:12, 0:64]),
        ):
            cp = pltpu.make_async_copy(src, dst, lsem.at[len(own)])
            cp.start()
            own.append(cp)

    barrier = pltpu.get_barrier_semaphore()

    def greet(dev):
        pl.semaphore_signal(barrier, inc=1, device_id=dev, device_id_type=MESH)

    greet(dev_p)
    greet(dev_m)
    for ok, dev in ((has_n, dev_n), (has_u, dev_u), (has_d, dev_d), (middle, dev_x)):

        @pl.when(ok)
        def _(dev=dev):
            greet(dev)

    zero2 = jnp.zeros((2, 2, CH, NZ), BF)

    @pl.when(jnp.logical_not(has_d))
    def _():
        ext[1:3, 0:2, 0:64, :] = zero2

    @pl.when(jnp.logical_not(has_u))
    def _():
        whole[:, 18:20] = zero2

    @pl.when(jnp.logical_not(has_n))
    def _():
        def clear(i, carry):
            ext[3, i] = jnp.zeros((2 * CH, NZ), BF)
            return carry

        lax.fori_loop(0, 12, clear, 0)

        def clear_res(i, carry):
            res[3, i] = jnp.zeros((2 * CH, NZ), BF)
            return carry

        lax.fori_loop(0, 10, clear_res, 0)

    for cp in own:
        cp.wait()
    pl.semaphore_wait(barrier, 2 + sum(ok.astype(jnp.int32) for ok in (has_n, has_u, has_d, middle)))

    counter = [0]
    sends = []

    def remote(src, dst, dev, ok=None, rok=None):
        k = counter[0]
        counter[0] += 1
        cp = pltpu.make_async_remote_copy(
            src_ref=src, dst_ref=dst, send_sem=ssem.at[k], recv_sem=rsem.at[k],
            device_id=dev, device_id_type=MESH,
        )
        rok = ok if rok is None else rok
        if ok is None:
            cp.start()
        else:
            pl.when(ok)(cp.start)
        sends.append((cp, ok))

        def arrived():
            if rok is None:
                cp.wait_recv()
            else:
                pl.when(rok)(cp.wait_recv)

        return arrived

    def k_rows(e, part):
        return ext.at[e, part[0] : part[0] + part[1], 0:64]

    def m_rows(e, part):
        return ext.at[e, part[0] : part[0] + part[1], 64:128]

    def to_n(rows, e, part):
        return remote(rows(e, part), rows(5 - e, part), dev_n, outer if rows is m_rows and e == 1 else has_n)

    def to_p(rows, part):
        return remote(rows(1, part), rows(0, part), dev_p)

    def to_x(part):
        first = 12 - part[0] - part[1]
        return remote(
            whole.at[0, 8 + first : 8 + first + part[1]],
            stage.at[2, first : first + part[1]],
            dev_x,
            middle,
        )

    def to_m(part):
        first = 12 - part[0] - part[1]
        return remote(
            whole.at[0:2, 8 + first : 8 + first + part[1]],
            stage.at[0:2, first : first + part[1]],
            dev_m,
        )

    from_d = remote(whole.at[0:2, 16:18], ext.at[1:3, 0:2, 0:64], dev_u, has_u, has_d)
    from_u = remote(whole.at[0:2, 2:4], whole.at[0:2, 18:20], dev_d, has_d, has_u)
    m_upper = to_m(UPPER)
    m_lower = to_m(LOWER)
    near = [to_n(k_rows, 2, MAIN)]
    p_k = to_p(k_rows, MAIN)
    x_far = [to_x(UPPER), to_x(LOWER)]

    build_weights(kernel_ref, wf, wa, side)
    row_id = lax.broadcasted_iota(jnp.int32, (NZ, NZ), 0)
    col_id = lax.broadcasted_iota(jnp.int32, (NZ, NZ), 1)
    flip[...] = jnp.where(row_id + col_id == NZ - 1, 1.0, 0.0).astype(BF)

    def turned(two):
        return jnp.dot(two.reshape(2 * CH, NZ), flip[...], preferred_element_type=F32)

    def turn(part, places=((0, 1), (1, 2))):
        start, count = part
        for slot, e in places:

            def pair(i, carry, slot=slot, e=e):
                t = start + 2 * i
                back = turned(stage[slot, pl.ds(10 - t, 2)]).astype(BF)
                ext[e, t, 64:128, :] = back[CH:]
                ext[e, t + 1, 64:128, :] = back[:CH]
                return carry

            lax.fori_loop(0, count // 2, pair, 0, unroll=count // 2)

    def planes(ref, e, row, which):
        return jnp.concatenate([ref[e + d, pl.ds(row, 3)].reshape(6 * CH, NZ) for d in which], axis=0)

    def summed(w, ref, e, row, which):
        first = (which[0] + 1) * 6 * CH
        terms = jnp.dot(
            w[:, first : first + len(which) * 6 * CH],
            planes(ref, e, row, which),
            preferred_element_type=F32,
        )
        return shift_sum(terms, 2 * CH)

    def rows_of(start, count, row):
        def step(i, carry):
            row(start + i)
            return carry

        lax.fori_loop(0, count, step, 0, unroll=count)

    def clear_edge(s, start):
        if start == 0:

            @pl.when(jnp.logical_not(has_d))
            def _():
                res[s + 1, 0] = jnp.zeros((2 * CH, NZ), BF)

    def forward(s, start, count):
        def row(j):
            total = summed(wf, ext, s + 1, j, (-1, 0, 1)) - ext[s + 1, j + 1].astype(F32)
            res[s + 1, j] = total.astype(BF)

        rows_of(start, count, row)
        clear_edge(s, start)

    def forward_early(start, count):
        def row(j):
            sum_f[j] = summed(wf, ext, 3, j, (-1, 0)) - ext[3, j + 1].astype(F32)

        rows_of(start, count, row)

    def forward_late(start, count):
        def row(j):
            res[3, j] = (sum_f[j] + summed(wf, ext, 3, j, (1,))).astype(BF)

        rows_of(start, count, row)
        clear_edge(2, start)

    def store_step(s, y, gradient):
        plane = plane_of(s)
        k = ext[s + 1, y + 2].astype(F32)
        keep = 1.0 - mask_ref[pl.ds(y, 1), :].astype(F32)
        new = k[:CH] - (STEP * keep) * gradient[:CH]
        upd_ref[plane, y] = new.astype(BF)
        out_ref[plane, y] = res[s + 1, y + 1, 0:64]
        step_m[s, y] = (k[CH:] - STEP * gradient[CH:]).astype(BF)

    def adjoint(start, count):
        def row(y):
            store_step(0, y, summed(wa, res, 1, y, (-1, 0, 1)) - res[1, y + 1].astype(F32))

        rows_of(start, count, row)

    def adjoint_early(start, count):
        def row(y):
            sum_a[y] = summed(wa, res, 2, y, (-1, 0)) - res[2, y + 1].astype(F32)

        rows_of(start, count, row)

    def adjoint_late(start, count):
        def row(y):
            store_step(1, y, sum_a[y] + summed(wa, res, 2, y, (1,)))

        rows_of(start, count, row)

    def return_r(s, start, count):
        return remote(
            res.at[s + 1, start + 1 : start + 1 + count, 64:128],
            back_r.at[s, start : start + count],
            dev_m,
        )

    def return_u(s, start, count):
        return remote(
            step_m.at[s, start : start + count], back_u.at[s, start : start + count], dev_m
        )

    def take_r(s, start, count):
        plane = plane_of(s)

        def pair(i, carry):
            q = start + 2 * i
            back = turned(back_r[s, pl.ds(q, 2)]).astype(BF)
            out_ref[plane, 15 - q] = back[:CH]
            out_ref[plane, 14 - q] = back[CH:]
            return carry

        lax.fori_loop(0, count // 2, pair, 0, unroll=count // 2)

    def take_u(s, start, count):
        plane = plane_of(s)

        def pair(i, carry):
            q = start + 2 * i
            back = turned(back_u[s, pl.ds(q, 2)])
            for n in (0, 1):
                y = 15 - q - n
                masked = jnp.broadcast_to(mask_ref[pl.ds(y, 1), :], (CH, NZ)) > 0
                k = whole[s, y + 2].astype(F32)
                upd_ref[plane, y] = jnp.where(masked, k, back[n * CH : n * CH + CH]).astype(BF)
            return carry

        lax.fori_loop(0, count // 2, pair, 0, unroll=count // 2)

    def when_n(fn, *args):
        pl.when(has_n)(lambda: fn(*args))

    from_d()
    near += [to_n(k_rows, 2, EDGE)]
    p_k_edge = to_p(k_rows, EDGE)
    from_u()
    m_edge = to_m(EDGE)
    x_far += [to_x(EDGE)]

    m_upper()
    turn(UPPER)
    near_upper = to_n(m_rows, 2, UPPER)
    p_upper = to_p(m_rows, UPPER)
    far = [to_n(k_rows, 1, MAIN)]
    m_lower()
    turn(LOWER)
    near_lower = to_n(m_rows, 2, LOWER)
    p_lower = to_p(m_rows, LOWER)
    p_k()
    p_upper()
    forward(0, 6, 4)
    r_0 = [return_r(0, 5, 3)]
    p_lower()
    forward(0, 2, 4)
    r_0 += [return_r(0, 1, 4)]
    m_edge()
    turn(EDGE)
    near_edge = to_n(m_rows, 2, EDGE)
    p_edge = to_p(m_rows, EDGE)
    far += [to_n(k_rows, 1, EDGE)]
    far_upper = to_n(m_rows, 1, UPPER)
    far_lower = to_n(m_rows, 1, LOWER)
    far_edge = to_n(m_rows, 1, EDGE)
    p_k_edge()
    p_edge()
    forward(0, 0, 2)
    r_p = remote(res.at[1], res.at[0], dev_p)
    r_0 += [return_r(0, 0, 1)]

    def direct(got, part):
        got()
        pl.when(middle)(lambda: turn(part, ((2, 4),)))

    for got in near:
        got()
    near_upper()
    forward(1, 6, 4)
    r_1 = [return_r(1, 5, 3)]
    r_p()
    adjoint(6, 2)
    u_0 = [return_u(0, 6, 2)]
    when_n(forward_early, 6, 4)
    near_lower()
    forward(1, 2, 4)
    r_1 += [return_r(1, 1, 4)]
    adjoint(2, 4)
    u_0 += [return_u(0, 2, 4)]
    when_n(forward_early, 2, 4)
    adjoint_early(2, 6)
    near_edge()
    forward(1, 0, 2)
    r_1 += [return_r(1, 0, 1)]
    adjoint(0, 2)
    u_0 += [return_u(0, 0, 2)]
    when_n(forward_early, 0, 2)
    adjoint_early(0, 2)
    for got in r_0:
        got()
    take_r(0, 0, 8)

    for got in far:
        got()
    far_upper()
    direct(x_far[0], UPPER)
    when_n(forward_late, 6, 4)
    adjoint_late(6, 2)
    u_1 = [return_u(1, 6, 2)]
    far_lower()
    direct(x_far[1], LOWER)
    when_n(forward_late, 2, 4)
    adjoint_late(2, 4)
    u_1 += [return_u(1, 2, 4)]
    far_edge()
    direct(x_far[2], EDGE)
    when_n(forward_late, 0, 2)
    adjoint_late(0, 2)
    u_1 += [return_u(1, 0, 2)]

    for got in r_1:
        got()
    take_r(1, 0, 8)
    for got in u_0:
        got()
    take_u(0, 0, 8)
    for got, start, count in zip(u_1, (6, 2, 0), (2, 4, 2)):
        got()
        take_u(1, start, count)
    for cp, ok in sends:
        if ok is None:
            cp.wait_send()
        else:
            pl.when(ok)(cp.wait_send)


N_COPIES = 40


def gradient_step(nx, ny, planes_first, kernel, mask):
    vmem = pl.BlockSpec(memory_space=pltpu.VMEM)
    shape = jax.ShapeDtypeStruct((2, ROWS, CH, NZ), BF)
    half = pltpu.VMEM((2, ROWS // 2, CH, NZ), BF)
    return pl.pallas_call(
        functools.partial(body, nx, ny),
        out_shape=(shape, shape),
        in_specs=[pl.BlockSpec(memory_space=pl.ANY), vmem, vmem],
        out_specs=(vmem, vmem),
        scratch_shapes=[
            pltpu.VMEM((5, 12, 2 * CH, NZ), BF),
            pltpu.VMEM((2, 20, CH, NZ), BF),
            pltpu.VMEM((3, 12, CH, NZ), BF),
            pltpu.VMEM((4, 10, 2 * CH, NZ), BF),
            pltpu.VMEM((10, 2 * CH, NZ), F32),
            pltpu.VMEM((8, 2 * CH, NZ), F32),
            half,
            half,
            half,
            pltpu.VMEM((6 * CH, 18 * CH), BF),
            pltpu.VMEM((6 * CH, 18 * CH), BF),
            pltpu.VMEM((NZ, NZ), BF),
            pltpu.SemaphoreType.DMA((4,)),
            pltpu.SemaphoreType.DMA((N_COPIES,)),
            pltpu.SemaphoreType.DMA((N_COPIES,)),
        ],
        compiler_params=pltpu.CompilerParams(
            collective_id=0, has_side_effects=True, vmem_limit_bytes=48 << 20
        ),
        name="gradient_step",
    )(planes_first, kernel, mask)


def local(nx, ny, kspace, kernel, mask):
    planes_first = jnp.transpose(kspace, (1, 2, 0, 3))
    updated, residual = gradient_step(nx, ny, planes_first, kernel, mask)
    return (
        jnp.transpose(updated, (2, 0, 1, 3)),
        jnp.transpose(residual, (2, 0, 1, 3)),
    )


def solution(mesh):
    nx, ny = mesh.shape["kx"], mesh.shape["ky"]
    return jax.shard_map(
        functools.partial(local, nx, ny),
        mesh=mesh,
        in_specs=(P(None, "kx", "ky", None), P(), P("ky", None)),
        out_specs=(P(None, "kx", "ky", None), P(None, "kx", "ky", None)),
        check_vma=False,
    )
```

```python
import functools

import jax
import jax.numpy as jnp
from jax import lax
from jax.experimental import pallas as pl
from jax.experimental.pallas import tpu as pltpu
from jax.sharding import PartitionSpec as P

MESH = pl.DeviceIdType.MESH
BF = jnp.bfloat16
F32 = jnp.float32
CH = 64
NZ = 256
ROWS = 16
STEP = 0.5


UPPER, LOWER, EDGE = (6, 6), (2, 4), (0, 2)
MAIN = (2, 10)


def shift_sum(terms, m):
    lane = lax.broadcasted_iota(jnp.int32, (m, NZ), 1)
    before = jnp.where(lane == 0, 0.0, pltpu.roll(terms[:m], 1, 1))
    after = jnp.where(lane == NZ - 1, 0.0, pltpu.roll(terms[2 * m :], NZ - 1, 1))
    return terms[m : 2 * m] + before + after


def build_weights(kernel_ref, wf, wa, side):
    lane = lax.broadcasted_iota(jnp.int32, (CH, 2 * CH), 1)
    sign = jnp.where(lane < CH + CH // 2, 1.0, -1.0)
    for i in range(3):
        plus, minus = 1 + side * (i - 1), 1 - side * (i - 1)
        for j in range(3):
            col = (i * 3 + j) * 2 * CH
            for l in range(3):
                here = kernel_ref[plus, j, l].astype(F32) * sign
                there = kernel_ref[minus, 2 - j, 2 - l].astype(F32) * sign
                wf[l * 128 : l * 128 + 64, col : col + 128] = here.astype(BF)
                wf[l * 128 + 64 : l * 128 + 128, col : col + 128] = pltpu.roll(there, CH, 1).astype(BF)
                both = jnp.concatenate([there, pltpu.roll(here, CH, 1)], axis=0)
                wa[l * 128 : l * 128 + 128, col : col + 128] = jnp.transpose(both).astype(BF)


def body(
    nx, ny, k_ref, kernel_ref, mask_ref, upd_ref, out_ref,
    ext, whole, stage, res, sum_f, sum_a, step_m, back_r, back_u, wf, wa, flip, lsem, ssem, rsem,
):
    a = lax.axis_index("kx")
    b = lax.axis_index("ky")
    core = lax.rem(a, 2)
    side = 2 * core - 1
    has_n = jnp.logical_and(a > 0, a < nx - 1)
    has_u = b < ny - 1
    has_d = b > 0
    dev_p = (a + 1 - 2 * core, b)
    dev_n = (jnp.clip(a + side, 0, nx - 1), b)
    dev_m = (nx - 1 - a, ny - 1 - b)
    middle = jnp.logical_or(a == nx // 2 - 1, a == nx // 2)
    outer = jnp.logical_and(has_n, jnp.logical_not(middle))
    dev_x = (nx - 1 - jnp.clip(a + side, 0, nx - 1), ny - 1 - b)
    dev_u = (a, jnp.minimum(b + 1, ny - 1))
    dev_d = (a, jnp.maximum(b - 1, 0))

    def plane_of(s):
        return (1 - s) + core * (2 * s - 1)

    own = []
    for s in (0, 1):
        for src, dst in (
            (k_ref.at[plane_of(s)], whole.at[s, 2:18]),
            (k_ref.at[plane_of(s), 0:10], ext.at[s + 1, 2:12, 0:64]),
        ):
            cp = pltpu.make_async_copy(src, dst, lsem.at[len(own)])
            cp.start()
            own.append(cp)

    barrier = pltpu.get_barrier_semaphore()

    def greet(dev):
        pl.semaphore_signal(barrier, inc=1, device_id=dev, device_id_type=MESH)

    greet(dev_p)
    greet(dev_m)
    for ok, dev in ((has_n, dev_n), (has_u, dev_u), (has_d, dev_d), (middle, dev_x)):

        @pl.when(ok)
        def _(dev=dev):
            greet(dev)

    zero2 = jnp.zeros((2, 2, CH, NZ), BF)

    @pl.when(jnp.logical_not(has_d))
    def _():
        ext[1:3, 0:2, 0:64, :] = zero2

    @pl.when(jnp.logical_not(has_u))
    def _():
        whole[:, 18:20] = zero2

    @pl.when(jnp.logical_not(has_n))
    def _():
        def clear(i, carry):
            ext[3, i] = jnp.zeros((2 * CH, NZ), BF)
            return carry

        lax.fori_loop(0, 12, clear, 0)

        def clear_res(i, carry):
            res[3, i] = jnp.zeros((2 * CH, NZ), BF)
            return carry

        lax.fori_loop(0, 10, clear_res, 0)

    for cp in own:
        cp.wait()
    pl.semaphore_wait(barrier, 2 + sum(ok.astype(jnp.int32) for ok in (has_n, has_u, has_d, middle)))

    counter = [0]
    sends = []

    def remote(src, dst, dev, ok=None, rok=None):
        k = counter[0]
        counter[0] += 1
        cp = pltpu.make_async_remote_copy(
            src_ref=src, dst_ref=dst, send_sem=ssem.at[k], recv_sem=rsem.at[k],
            device_id=dev, device_id_type=MESH,
        )
        rok = ok if rok is None else rok
        if ok is None:
            cp.start()
        else:
            pl.when(ok)(cp.start)
        sends.append((cp, ok))

        def arrived():
            if rok is None:
                cp.wait_recv()
            else:
                pl.when(rok)(cp.wait_recv)

        return arrived

    def k_rows(e, part):
        return ext.at[e, part[0] : part[0] + part[1], 0:64]

    def m_rows(e, part):
        return ext.at[e, part[0] : part[0] + part[1], 64:128]

    def to_n(rows, e, part):
        return remote(rows(e, part), rows(5 - e, part), dev_n, outer if rows is m_rows else has_n)

    def to_p(rows, part):
        return remote(rows(1, part), rows(0, part), dev_p)

    def to_x(part, s=1):
        first = 12 - part[0] - part[1]
        return remote(
            whole.at[s, 8 + first : 8 + first + part[1]],
            stage.at[3 - s, first : first + part[1]],
            dev_x,
            middle,
        )

    def to_m(part):
        first = 12 - part[0] - part[1]
        return remote(
            whole.at[0:2, 8 + first : 8 + first + part[1]],
            stage.at[0:2, first : first + part[1]],
            dev_m,
        )

    from_d = remote(whole.at[0:2, 16:18], ext.at[1:3, 0:2, 0:64], dev_u, has_u, has_d)
    from_u = remote(whole.at[0:2, 2:4], whole.at[0:2, 18:20], dev_d, has_d, has_u)
    m_upper = to_m(UPPER)
    m_lower = to_m(LOWER)
    near = [to_n(k_rows, 2, MAIN)]
    p_k = to_p(k_rows, MAIN)
    x_far = [to_x(UPPER), to_x(LOWER)]

    build_weights(kernel_ref, wf, wa, side)
    row_id = lax.broadcasted_iota(jnp.int32, (NZ, NZ), 0)
    col_id = lax.broadcasted_iota(jnp.int32, (NZ, NZ), 1)
    flip[...] = jnp.where(row_id + col_id == NZ - 1, 1.0, 0.0).astype(BF)

    def turned(two):
        return jnp.dot(two.reshape(2 * CH, NZ), flip[...], preferred_element_type=F32)

    def turn(part, places=((0, 1), (1, 2))):
        start, count = part
        for slot, e in places:

            def pair(i, carry, slot=slot, e=e):
                t = start + 2 * i
                back = turned(stage[slot, pl.ds(10 - t, 2)]).astype(BF)
                ext[e, t, 64:128, :] = back[CH:]
                ext[e, t + 1, 64:128, :] = back[:CH]
                return carry

            lax.fori_loop(0, count // 2, pair, 0, unroll=count // 2)

    def planes(ref, e, row, which):
        return jnp.concatenate([ref[e + d, pl.ds(row, 3)].reshape(6 * CH, NZ) for d in which], axis=0)

    def summed(w, ref, e, row, which):
        first = (which[0] + 1) * 6 * CH
        terms = jnp.dot(
            w[:, first : first + len(which) * 6 * CH],
            planes(ref, e, row, which),
            preferred_element_type=F32,
        )
        return shift_sum(terms, 2 * CH)

    def rows_of(start, count, row):
        def step(i, carry):
            row(start + i)
            return carry

        lax.fori_loop(0, count, step, 0, unroll=count)

    def clear_edge(s, start):
        if start == 0:

            @pl.when(jnp.logical_not(has_d))
            def _():
                res[s + 1, 0] = jnp.zeros((2 * CH, NZ), BF)

    def forward(s, start, count):
        def row(j):
            total = summed(wf, ext, s + 1, j, (-1, 0, 1)) - ext[s + 1, j + 1].astype(F32)
            res[s + 1, j] = total.astype(BF)

        rows_of(start, count, row)
        clear_edge(s, start)

    def forward_early(start, count):
        def row(j):
            sum_f[j] = summed(wf, ext, 3, j, (-1, 0)) - ext[3, j + 1].astype(F32)

        rows_of(start, count, row)

    def forward_late(start, count):
        def row(j):
            res[3, j] = (sum_f[j] + summed(wf, ext, 3, j, (1,))).astype(BF)

        rows_of(start, count, row)
        clear_edge(2, start)

    def store_step(s, y, gradient):
        plane = plane_of(s)
        k = ext[s + 1, y + 2].astype(F32)
        keep = 1.0 - mask_ref[pl.ds(y, 1), :].astype(F32)
        new = k[:CH] - (STEP * keep) * gradient[:CH]
        upd_ref[plane, y] = new.astype(BF)
        out_ref[plane, y] = res[s + 1, y + 1, 0:64]
        step_m[s, y] = (k[CH:] - STEP * gradient[CH:]).astype(BF)

    def adjoint(start, count):
        def row(y):
            store_step(0, y, summed(wa, res, 1, y, (-1, 0, 1)) - res[1, y + 1].astype(F32))

        rows_of(start, count, row)

    def adjoint_early(start, count):
        def row(y):
            sum_a[y] = summed(wa, res, 2, y, (-1, 0)) - res[2, y + 1].astype(F32)

        rows_of(start, count, row)

    def adjoint_late(start, count):
        def row(y):
            store_step(1, y, sum_a[y] + summed(wa, res, 2, y, (1,)))

        rows_of(start, count, row)

    def return_r(s, start, count):
        return remote(
            res.at[s + 1, start + 1 : start + 1 + count, 64:128],
            back_r.at[s, start : start + count],
            dev_m,
        )

    def return_u(s, start, count):
        return remote(
            step_m.at[s, start : start + count], back_u.at[s, start : start + count], dev_m
        )

    def take_r(s, start, count):
        plane = plane_of(s)

        def pair(i, carry):
            q = start + 2 * i
            back = turned(back_r[s, pl.ds(q, 2)]).astype(BF)
            out_ref[plane, 15 - q] = back[:CH]
            out_ref[plane, 14 - q] = back[CH:]
            return carry

        lax.fori_loop(0, count // 2, pair, 0, unroll=count // 2)

    def take_u(s, start, count):
        plane = plane_of(s)

        def pair(i, carry):
            q = start + 2 * i
            back = turned(back_u[s, pl.ds(q, 2)])
            for n in (0, 1):
                y = 15 - q - n
                masked = jnp.broadcast_to(mask_ref[pl.ds(y, 1), :], (CH, NZ)) > 0
                k = whole[s, y + 2].astype(F32)
                upd_ref[plane, y] = jnp.where(masked, k, back[n * CH : n * CH + CH]).astype(BF)
            return carry

        lax.fori_loop(0, count // 2, pair, 0, unroll=count // 2)

    def when_n(fn, *args):
        pl.when(has_n)(lambda: fn(*args))

    from_d()
    near += [to_n(k_rows, 2, EDGE)]
    p_k_edge = to_p(k_rows, EDGE)
    from_u()
    m_edge = to_m(EDGE)
    x_far += [to_x(EDGE)]

    m_upper()
    turn(UPPER)
    near_upper = to_n(m_rows, 2, UPPER)
    p_upper = to_p(m_rows, UPPER)
    far = [to_n(k_rows, 1, MAIN)]
    m_lower()
    turn(LOWER)
    near_lower = to_n(m_rows, 2, LOWER)
    p_lower = to_p(m_rows, LOWER)
    p_k()
    p_upper()
    forward(0, 6, 4)
    r_0 = [return_r(0, 5, 3)]
    p_lower()
    forward(0, 2, 4)
    r_0 += [return_r(0, 1, 4)]
    m_edge()
    turn(EDGE)
    near_edge = to_n(m_rows, 2, EDGE)
    p_edge = to_p(m_rows, EDGE)
    far += [to_n(k_rows, 1, EDGE)]
    x_last = [to_x(UPPER, 0), to_x(LOWER, 0), to_x(EDGE, 0)]
    far_upper = to_n(m_rows, 1, UPPER)
    far_lower = to_n(m_rows, 1, LOWER)
    far_edge = to_n(m_rows, 1, EDGE)
    p_k_edge()
    p_edge()
    forward(0, 0, 2)
    r_p = remote(res.at[1], res.at[0], dev_p)
    r_0 += [return_r(0, 0, 1)]

    def direct(got, part, slot=2):
        got()
        pl.when(middle)(lambda: turn(part, ((slot, slot + 1),)))

    for got in near:
        got()
    near_upper()
    direct(x_far[0], UPPER)
    forward(1, 6, 4)
    r_1 = [return_r(1, 5, 3)]
    r_p()
    adjoint(6, 2)
    u_0 = [return_u(0, 6, 2)]
    when_n(forward_early, 6, 4)
    near_lower()
    direct(x_far[1], LOWER)
    forward(1, 2, 4)
    r_1 += [return_r(1, 1, 4)]
    adjoint(2, 4)
    u_0 += [return_u(0, 2, 4)]
    when_n(forward_early, 2, 4)
    adjoint_early(2, 6)
    near_edge()
    direct(x_far[2], EDGE)
    forward(1, 0, 2)
    r_1 += [return_r(1, 0, 1)]
    adjoint(0, 2)
    u_0 += [return_u(0, 0, 2)]
    when_n(forward_early, 0, 2)
    adjoint_early(0, 2)
    for got in r_0:
        got()
    take_r(0, 0, 8)

    for got in far:
        got()
    far_upper()
    direct(x_last[0], UPPER, 3)
    when_n(forward_late, 6, 4)
    adjoint_late(6, 2)
    u_1 = [return_u(1, 6, 2)]
    far_lower()
    direct(x_last[1], LOWER, 3)
    when_n(forward_late, 2, 4)
    adjoint_late(2, 4)
    u_1 += [return_u(1, 2, 4)]
    far_edge()
    direct(x_last[2], EDGE, 3)
    when_n(forward_late, 0, 2)
    adjoint_late(0, 2)
    u_1 += [return_u(1, 0, 2)]

    for got in r_1:
        got()
    take_r(1, 0, 8)
    for got in u_0:
        got()
    take_u(0, 0, 8)
    for got, start, count in zip(u_1, (6, 2, 0), (2, 4, 2)):
        got()
        take_u(1, start, count)
    for cp, ok in sends:
        if ok is None:
            cp.wait_send()
        else:
            pl.when(ok)(cp.wait_send)


N_COPIES = 40


def gradient_step(nx, ny, planes_first, kernel, mask):
    vmem = pl.BlockSpec(memory_space=pltpu.VMEM)
    shape = jax.ShapeDtypeStruct((2, ROWS, CH, NZ), BF)
    half = pltpu.VMEM((2, ROWS // 2, CH, NZ), BF)
    return pl.pallas_call(
        functools.partial(body, nx, ny),
        out_shape=(shape, shape),
        in_specs=[pl.BlockSpec(memory_space=pl.ANY), vmem, vmem],
        out_specs=(vmem, vmem),
        scratch_shapes=[
            pltpu.VMEM((5, 12, 2 * CH, NZ), BF),
            pltpu.VMEM((2, 20, CH, NZ), BF),
            pltpu.VMEM((4, 12, CH, NZ), BF),
            pltpu.VMEM((4, 10, 2 * CH, NZ), BF),
            pltpu.VMEM((10, 2 * CH, NZ), F32),
            pltpu.VMEM((8, 2 * CH, NZ), F32),
            half,
            half,
            half,
            pltpu.VMEM((6 * CH, 18 * CH), BF),
            pltpu.VMEM((6 * CH, 18 * CH), BF),
            pltpu.VMEM((NZ, NZ), BF),
            pltpu.SemaphoreType.DMA((4,)),
            pltpu.SemaphoreType.DMA((N_COPIES,)),
            pltpu.SemaphoreType.DMA((N_COPIES,)),
        ],
        compiler_params=pltpu.CompilerParams(
            collective_id=0, has_side_effects=True, vmem_limit_bytes=48 << 20
        ),
        name="gradient_step",
    )(planes_first, kernel, mask)


def local(nx, ny, kspace, kernel, mask):
    planes_first = jnp.transpose(kspace, (1, 2, 0, 3))
    updated, residual = gradient_step(nx, ny, planes_first, kernel, mask)
    return (
        jnp.transpose(updated, (2, 0, 1, 3)),
        jnp.transpose(residual, (2, 0, 1, 3)),
    )


def solution(mesh):
    nx, ny = mesh.shape["kx"], mesh.shape["ky"]
    return jax.shard_map(
        functools.partial(local, nx, ny),
        mesh=mesh,
        in_specs=(P(None, "kx", "ky", None), P(), P("ky", None)),
        out_specs=(P(None, "kx", "ky", None), P(None, "kx", "ky", None)),
        check_vma=False,
    )
```
